32 devices in a mesh: sub: 8 (over z, y), split: 4 (over x, core).
Axes of the slice: x: 2, y: 2, z: 4, core: 2. Of those that a mesh axis runs over, the one named last changes fastest.
Arguments:
- stiffness: bfloat16 [8, 16, 10, 128, 128], P('sub', 'split'), may hold values from -4.2 to 4.2
- pattern: int32 [8, 16, 10], P('sub', 'split'), may hold values from 0 to 15, as said below
- mass: float32 [8, 2048], P('sub', 'split'), may hold values from 0.5 to 2
- start_modes: bfloat16 [8, 2048, 128], P('sub', 'split'), may hold values from -6 to 6
- cut_low: float32 [8], P('sub'), may hold values from 2 to 3
- cut_high: float32 [8], P('sub'), may hold values from 11 to 13
- coupling: bfloat16 [8, 8, 128, 2048], P('sub', None, None, 'split'), may hold values from -0.29882812 to 0.29882812
- incidence: int32 [8, 8], P('sub'), may hold values from 0 to 7, all different within a row
- slot_of: int32 [8], replicated, may hold values from 0 to 7, each once
Outputs:
- reduced: float32 [8, 128, 128], P('sub', 'split')
- ritz: float32 [8, 128], P('sub')
The draws below stay inside these ranges and needn't reach their ends.
Inputs may be any that keep to these rules, and one draw needn't show every extreme that they name: pattern[s, i, 0] == i; the 10 block columns of a block row are distinct. `incidence`: each row names 8 distinct interface blocks and every interface block is named by some row. `slot_of`: a permutation.
All inputs are finite; a program needn't handle non-finite values.
Results may differ from the reference program's by a relative error of at most 0.011.
Values may be sent and summed in bfloat16 or wider, within the bound.
No kernel may reach another device: no remote copies, remote signals or barrier semaphores. Data moves between devices by JAX's collectives and lax.ppermute only.
A program may use at most 64 MiB of HBM per device.

```python
import math
import jax
import jax.numpy as jnp
from jax import lax

BS = 128
MODES = 128
NZB = 10
NIF = 8
DEG = 4
ITERS = 2
SUBS = 8
NB = 16
NDOF = 2048
IFACES = 8


def draw_pattern(key, part):
    key = jax.random.fold_in(key, 11)
    count = SUBS * NB
    keys = jax.random.split(key, count)
    perms = jax.vmap(lambda k: jax.random.permutation(k, NB - 1))(keys)[:, :NZB - 1]
    own = jnp.arange(count, dtype=jnp.int32) % NB
    rest = (own[:, None] + 1 + perms.astype(jnp.int32)) % NB
    return jnp.concatenate([own[:, None], rest], axis=1).reshape(SUBS, NB, NZB).astype(jnp.int32)


def draw_stiffness(key, part):
    key = jax.random.fold_in(key, 12)
    first, second = jax.random.split(key)
    shape = (SUBS, NB, NZB, BS, BS)
    base = jnp.clip(0.02 * jax.random.normal(first, shape, jnp.float32), -0.1, 0.1)
    lift = jax.random.uniform(second, (SUBS, NB, 1, BS, 1), jnp.float32, 2.0, 4.0)
    eye = (jnp.arange(BS)[:, None] == jnp.arange(BS)[None, :]).astype(jnp.float32)
    first_slot = (jnp.arange(NZB) == 0).astype(jnp.float32)
    values = base + lift * eye[None, None, None, :, :] * first_slot[None, None, :, None, None]
    return values.astype(jnp.bfloat16)


def levels(stream_key, extent, pieces, low, high):
    def one(axis_at, shards_of):
        draws = jax.random.uniform(jax.random.fold_in(jax.random.fold_in(stream_key, 6), axis_at), (shards_of,), jnp.float32, low / len(pieces), high / len(pieces))
        return jnp.repeat(jnp.exp(draws), extent[axis_at] // shards_of).reshape((-1,) + (1,) * (len(extent) - axis_at - 1))

    loudness = one(*pieces[0])
    for cut in pieces[1:]:
        loudness = loudness * one(*cut)
    return loudness


def distinct(key, rows, count, top, lift):
    order = jax.random.permutation(jax.random.fold_in(key, 1), count)
    pull = order
    for power in range(3):
        pull = pull * pull // count
    pull = pull * lift // count
    tickets = jax.random.randint(jax.random.fold_in(key, 2), (rows, count), 0, 4096) + pull
    sure = jax.random.permutation(jax.random.fold_in(key, 3), rows)[jnp.arange(count) % rows]
    tickets = jnp.where(jnp.arange(rows)[:, None] == sure[None, :], 1 << 14, tickets)
    score = tickets * count + jnp.arange(count)
    return lax.top_k(score.astype(jnp.int32), top)[1].astype(jnp.int32)


def bell_draw(own_key, extent, deviation, reach, shards=(), held_as=jnp.bfloat16):
    factor_of = levels(own_key, extent, shards, -0.22, 0.18) if shards else 1.0
    values = jax.random.normal(own_key, extent, jnp.float32) * deviation * factor_of
    return jnp.minimum(jnp.maximum(values, -reach), reach).astype(held_as)


def setup_inputs(seed: int = 0) -> dict:
    streams_of = jax.random.split(jax.random.key(seed), 10)
    return {
        "stiffness": draw_stiffness(jax.random.fold_in(streams_of[9], 71), 0),
        "pattern": draw_pattern(jax.random.fold_in(streams_of[9], 71), 0),
        "mass": jnp.clip(jnp.exp(math.log(2.0) - 1.3862944 * jax.random.uniform(streams_of[2], (SUBS, NDOF), jnp.float32) ** levels(streams_of[2], (SUBS, NDOF), ((0, 8), (1, 4)), -0.2, 0.2)), 0.5, 2.0),
        "start_modes": bell_draw(streams_of[3], (SUBS, NDOF, MODES), 1.0, 6.0, ((0, 8), (1, 4))),
        "cut_low": jnp.clip(2.0 + 1.0 * jax.random.uniform(streams_of[4], (SUBS,), jnp.float32) ** levels(streams_of[4], (SUBS,), ((0, 8),), -0.2, 0.2), 2.0, 3.0),
        "cut_high": jnp.clip(11.0 + 2.0 * jax.random.uniform(streams_of[5], (SUBS,), jnp.float32) ** levels(streams_of[5], (SUBS,), ((0, 8),), -0.2, 0.2), 11.0, 13.0),
        "coupling": bell_draw(streams_of[6], (SUBS, NIF, BS, NDOF), 0.05, 0.29882812, ((0, 8), (3, 4))),
        "incidence": distinct(streams_of[7], SUBS, IFACES, NIF, 12000),
        "slot_of": jax.random.permutation(streams_of[8], IFACES).astype(jnp.int32),
    }


HIGH = lax.Precision.HIGHEST

def stiff_apply(stiff, pat, field):
    blocks = field.reshape(NB, BS, MODES)[pat]
    prod = jnp.einsum('rkab,rkbm->ram', stiff.astype(jnp.float32), blocks.astype(jnp.float32), precision=HIGH)
    return prod.reshape(NDOF, MODES)

def one_substructure(inputs):
    stiff, pat, weight, phi, low_end, high_end, kgi = inputs
    centre = (high_end + low_end) / 2.0
    half = (high_end - low_end) / 2.0
    for outer in range(ITERS):
        prev = phi
        image = stiff_apply(stiff, pat, phi) / weight[:, None]
        cur = ((image - centre * phi.astype(jnp.float32)) / half).astype(jnp.bfloat16)
        for inner in range(DEG - 1):
            image = stiff_apply(stiff, pat, cur) / weight[:, None]
            nxt = (2.0 * (image - centre * cur.astype(jnp.float32)) / half - prev.astype(jnp.float32)).astype(jnp.bfloat16)
            prev, cur = (cur, nxt)
        filtered = cur.astype(jnp.float32)
        gram = jnp.dot((filtered * weight[:, None]).T, filtered, precision=HIGH)
        lower = jnp.linalg.cholesky(gram)
        phi = lax.linalg.triangular_solve(lower, filtered, left_side=False, lower=True, transpose_a=True).astype(jnp.bfloat16)
    phif = phi.astype(jnp.float32)
    theta = lax.optimization_barrier(jnp.sum(phif * stiff_apply(stiff, pat, phi), axis=0))
    prods = jnp.einsum('ibr,rm->ibm', kgi.astype(jnp.float32), phif, precision=HIGH)
    scaled = prods * lax.rsqrt(theta)[None, None, :]
    items = jnp.einsum('iam,ibm->iab', scaled, scaled, precision=HIGH)
    return (theta, items)

def reference(stiffness, pattern, mass, start_modes, cut_low, cut_high, coupling, incidence, slot_of):
    theta, items = lax.map(one_substructure, (stiffness, pattern, mass, start_modes, cut_low, cut_high, coupling))
    targets = slot_of[incidence].reshape(-1).astype(jnp.int32)
    reduced = jax.ops.segment_sum(items.reshape(SUBS * NIF, BS, BS), targets, num_segments=IFACES)
    return (reduced, theta)
```

```python
import functools

import jax
import jax.numpy as jnp
from jax import lax
from jax.experimental import pallas as pl
from jax.experimental.pallas import tpu as pltpu
from jax.sharding import PartitionSpec as P

DEG = 4
ITERS = 2
F32 = jnp.float32
BF16 = jnp.bfloat16


def split2(x):
    hi = x.astype(BF16)
    return hi, (x - hi.astype(F32)).astype(BF16)


def inverse_factor(gram):
    n = gram.shape[0]
    lane = lax.broadcasted_iota(jnp.int32, (8, n), 1)
    sub = lax.broadcasted_iota(jnp.int32, (8, n), 0)
    groups = n // 8
    rows = [gram[8 * g : 8 * g + 8, :] for g in range(groups)]
    for j in range(n):
        gj, sj = divmod(j, 8)
        row = rows[gj][sj : sj + 1, :]
        pivot = jnp.broadcast_to(row[:, j : j + 1], (8, n))
        inv = 1.0 / pivot
        at = lane == j
        unit = jnp.where(at, 1.0, jnp.broadcast_to(row, (8, n)))
        scaled = unit * inv
        for g in range(gj, groups):
            col = jnp.broadcast_to(rows[g][:, j : j + 1], (8, n))
            if g == gj:
                if sj == 7:
                    continue
                below = sub > sj
                rows[g] = jnp.where(below, jnp.where(at, 0.0, rows[g]) - col * scaled, rows[g])
            else:
                rows[g] = jnp.where(at, 0.0, rows[g]) - col * scaled
    out = []
    for g in range(groups):
        here = lane == sub + 8 * g
        diag = jnp.sum(jnp.where(here, rows[g], 0.0), axis=1, keepdims=True)
        lower = jnp.where(lane < sub + 8 * g, rows[g], jnp.where(here, 1.0, 0.0))
        out.append(lower * lax.rsqrt(diag))
    return jnp.concatenate(out, axis=0).T


def filter_kernel(nranks, pat, rank, ends, mass, k0, k1, k2, k3, y0, y1, y2, y3, phi_out, theta_out, stiff, ya, yb, scale, ksem, ysem):
    nb, nzb = pat.shape
    bs = stiff.shape[-1]
    own = nb // nranks
    me = rank[0]
    copies = []
    for t, ref in enumerate((y0, y1, y2, y3)):
        at = pl.multiple_of((me ^ t) * (own * bs), own * bs)
        copies.append(pltpu.make_async_copy(ref, ya.at[pl.ds(at, own * bs)], ysem.at[t]))
        copies[-1].start()
    kcopies = []
    for t, ref in enumerate((k0, k1, k2, k3)):
        kcopies.append(pltpu.make_async_copy(ref, stiff.at[pl.ds((me ^ t) * own, own)], ksem.at[t]))
        kcopies[-1].start()
    centre = (ends[1] + ends[0]) / 2.0
    half = (ends[1] - ends[0]) / 2.0
    for i in range(nb):
        row = jnp.broadcast_to(mass[i : i + 1, :], (bs, bs)).T
        scale[i * bs : (i + 1) * bs, :] = 1.0 / (row * half)
    shift = jnp.full((1, 1), centre, F32) / half
    for c in copies:
        c.wait()

    def image(i, src):
        left = jnp.concatenate([stiff[i, k] for k in range(nzb)], axis=1)
        right = jnp.concatenate(
            [src[pl.ds(pl.multiple_of(pat[i, k] * bs, bs), bs), :] for k in range(nzb)], axis=0
        )
        return jnp.dot(left, right, preferred_element_type=F32)

    def rows_of(i):
        return pl.ds(pl.multiple_of(i * bs, bs), bs)

    def first(i):
        at = rows_of(i)
        yb[at, :] = (image(i, ya) * scale[at, :] - shift * ya[at, :].astype(F32)).astype(BF16)

    def later(i, src, dst):
        at = rows_of(i)
        dst[at, :] = (
            2.0 * (image(i, src) * scale[at, :] - shift * src[at, :].astype(F32)) - dst[at, :].astype(F32)
        ).astype(BF16)

    step = 2

    def sweep(body):
        @pl.loop(0, nb, step=step)
        def _(i):
            for u in range(step):
                body(i + u)

    def finish():
        src, dst = yb, ya
        for _ in range(DEG - 1):
            sweep(lambda i, src=src, dst=dst: later(i, src, dst))
            src, dst = dst, src
        cur = src
        gram = jnp.zeros((bs, bs), F32)
        for i in range(nb):
            blk = cur[i * bs : (i + 1) * bs, :]
            row = jnp.broadcast_to(mass[i : i + 1, :], (bs, bs)).T
            hi, lo = split2(blk.astype(F32) * row)
            both = lax.dot_general(
                blk, jnp.concatenate([hi, lo], axis=1), (((0,), (0,)), ((), ())), preferred_element_type=F32
            )
            gram = gram + both[:, :bs] + both[:, bs:]
        hi, lo = split2(inverse_factor(gram))
        weights = jnp.concatenate([hi, lo], axis=0)
        for i in range(nb):
            blk = cur[i * bs : (i + 1) * bs, :]
            ya[i * bs : (i + 1) * bs, :] = jnp.dot(
                jnp.concatenate([blk, blk], axis=1), weights, preferred_element_type=F32
            ).astype(BF16)

    @pl.loop(0, ITERS)
    def _(it):
        for t in range(nranks):

            @pl.when(it == 0)
            def _(t=t):
                kcopies[t].wait()

            base = (me ^ t) * own
            for r in range(own):
                first(base + r)
        finish()

    theta_out[...] = jnp.zeros_like(theta_out)

    @pl.loop(0, nb, step=step)
    def _(i):
        for u in range(step):
            at = rows_of(i + u)
            prod = ya[at, :].astype(F32) * image(i + u, ya)
            theta_out[...] += jnp.sum(prod, axis=0, keepdims=True)

    phi_out[...] = ya[...]


def face_kernel(nranks, rank, targets, theta, phi, c0, c1, c2, c3, keep, send):
    me = rank[0]
    njs, bs, cols = c0.shape
    faces, share = keep.shape[0], keep.shape[1]
    keep[...] = jnp.zeros_like(keep)
    send[...] = jnp.zeros_like(send)
    rs = lax.rsqrt(theta[...])
    for j in range(njs):
        prod = jnp.zeros((bs, bs), F32)
        for t, ref in enumerate((c0, c1, c2, c3)):
            at = pl.multiple_of((me ^ t) * cols, cols)
            prod = prod + jnp.dot(ref[j], phi[pl.ds(at, cols), :], preferred_element_type=F32)
        hi, lo = split2(prod * rs)
        left = jnp.concatenate([hi, lo, hi], axis=1)
        right = jnp.concatenate([hi, hi, lo], axis=1)
        item = lax.dot_general(left, right, (((1,), (1,)), ((), ())), preferred_element_type=F32)
        pieces = [item[share * r : share * (r + 1), :] for r in range(nranks)]
        mine = pieces[0]
        other = pieces[0]
        for r in range(1, nranks):
            mine = jnp.where(me == r, pieces[r], mine)
            other = jnp.where((me ^ 1) == r, pieces[r], other)
        keep[targets[j]] = mine
        send[targets[j]] = other.astype(BF16)


def shards(stiffness, pattern, mass, start_modes, cut_low, cut_high, coupling, incidence, slot_of):
    stiff = stiffness[0]
    own, nzb, bs, _ = stiff.shape
    modes = start_modes.shape[-1]
    nranks = lax.axis_size("split")
    nsub = lax.axis_size("sub")
    me = lax.axis_index("split")
    sub = lax.axis_index("sub")
    nb = own * nranks
    faces = slot_of.shape[0]
    nif = coupling.shape[1]
    assert nranks == 4 and nsub & (nsub - 1) == 0

    def swap(x, bits, axis="split", n=nranks):
        return lax.ppermute(x, axis, [(i, i ^ bits) for i in range(n)])

    y_x = swap(start_modes[0], 2)
    small = jnp.concatenate(
        [mass[0].reshape(-1, 128), jnp.pad(pattern[0].astype(F32).reshape(1, -1), ((0, 0), (0, 128 - own * nzb)))], axis=0
    )
    s_x = swap(small, 2)
    k_x = swap(stiff, 2)
    y_c = swap(start_modes[0], 1)
    s_c = swap(small, 1)
    k_c = swap(stiff, 1)
    s_d = swap(s_x, 1)
    y_d = swap(y_x, 1)
    k_d = swap(k_x, 1)

    halfj = nif // 2
    parity = me % 2
    coup = coupling[0]
    same = lax.dynamic_slice_in_dim(coup, parity * halfj, halfj, 0)
    other = lax.dynamic_slice_in_dim(coup, (1 - parity) * halfj, halfj, 0)
    g_x = swap(same, 2)
    g_d = swap(other, 3)
    g_c = swap(other, 1)

    smalls = jnp.stack([small, s_c, s_x, s_d])[jnp.arange(nranks) ^ me]
    mass_all = smalls[:, :-1].reshape(nb, bs)
    pat_all = smalls[:, -1, : own * nzb].astype(jnp.int32).reshape(nb, nzb)
    ends = jnp.concatenate([cut_low, cut_high])
    rank = me.astype(jnp.int32).reshape(1)

    smem = pl.BlockSpec(memory_space=pltpu.SMEM)
    vmem = pl.BlockSpec(memory_space=pltpu.VMEM)
    hbm = pl.BlockSpec(memory_space=pl.ANY)
    phi, theta = pl.pallas_call(
        functools.partial(filter_kernel, nranks),
        out_shape=(
            jax.ShapeDtypeStruct((nb * bs, modes), BF16),
            jax.ShapeDtypeStruct((1, modes), F32),
        ),
        in_specs=[smem, smem, smem, vmem] + [hbm] * 8,
        out_specs=(vmem, vmem),
        scratch_shapes=[
            pltpu.VMEM((nb, nzb, bs, bs), BF16),
            pltpu.VMEM((nb * bs, modes), BF16),
            pltpu.VMEM((nb * bs, modes), BF16),
            pltpu.VMEM((nb * bs, modes), F32),
            pltpu.SemaphoreType.DMA((4,)),
            pltpu.SemaphoreType.DMA((4,)),
        ],
        compiler_params=pltpu.CompilerParams(vmem_limit_bytes=40 << 20),
        name="filter",
    )(pat_all, rank, ends, mass_all, stiff, k_c, k_x, k_d, start_modes[0], y_c, y_x, y_d)

    links = lax.dynamic_slice_in_dim(incidence[0], parity * halfj, halfj, 0)
    targets = slot_of[links] ^ (sub * (faces // nsub))
    share = bs // nranks
    keep, send = pl.pallas_call(
        functools.partial(face_kernel, nranks),
        out_shape=(
            jax.ShapeDtypeStruct((faces, share, bs), F32),
            jax.ShapeDtypeStruct((faces, share, bs), BF16),
        ),
        in_specs=[smem, smem, vmem, vmem] + [vmem] * 4,
        out_specs=(vmem, vmem),
        compiler_params=pltpu.CompilerParams(vmem_limit_bytes=40 << 20),
        name="faces",
    )(rank, targets, theta, phi, same, g_c, g_x, g_d)
    total = keep + swap(send, 1).astype(F32)
    width = nsub // 2
    per = faces // nsub
    while width:
        lo, hi = total[: width * per], total[width * per :]
        total = lo + swap(hi.astype(BF16), width, "sub", nsub).astype(F32)
        width //= 2
    return (total, theta)


def solution(mesh):
    placed = (
        P("sub", "split", None, None, None),
        P("sub", "split", None),
        P("sub", "split"),
        P("sub", "split", None),
        P("sub"),
        P("sub"),
        P("sub", None, None, "split"),
        P("sub", None),
        P(),
    )
    return jax.shard_map(
        shards,
        mesh=mesh,
        in_specs=placed,
        out_specs=(P("sub", "split", None), P("sub", None)),
        check_vma=False,
    )
```

```python
import functools

import jax
import jax.numpy as jnp
from jax import lax
from jax.experimental import pallas as pl
from jax.experimental.pallas import tpu as pltpu
from jax.sharding import PartitionSpec as P

DEG = 4
ITERS = 2
F32 = jnp.float32
BF16 = jnp.bfloat16
GATE_VMEM = 24 << 20
FILTER_VMEM = 24 << 20


def split2(x):
    hi = x.astype(BF16)
    return hi, (x - hi.astype(F32)).astype(BF16)


def inverse_factor(gram):
    n = gram.shape[0]
    lane = lax.broadcasted_iota(jnp.int32, (8, n), 1)
    sub = lax.broadcasted_iota(jnp.int32, (8, n), 0)
    groups = n // 8
    w = [gram[8 * g : 8 * g + 8, :] for g in range(groups)]

    def spread(x):
        return jnp.broadcast_to(x, (8, n))

    for b in range(groups):
        j0 = 8 * b
        inside = (lane >= j0) & (lane < j0 + 8)
        cols = [{g: spread(w[g][:, j0 + c : j0 + c + 1]) for g in range(b, groups)} for c in range(8)]
        z = jnp.where(inside, jnp.where(lane == sub + j0, 1.0, 0.0), w[b])
        for g in range(b + 1, groups):
            w[g] = jnp.where(inside, 0.0, w[g])
        pivots = jnp.ones((8, n), F32)
        for c in range(8):
            pivot = spread(cols[c][b][c : c + 1, :])
            inv = 1.0 / pivot
            pivots = jnp.where(sub == c, pivot, pivots)
            mult = {g: cols[c][g] * inv for g in range(b + 1, groups)}
            if c < 7:
                mult[b] = jnp.where(sub > c, cols[c][b] * inv, 0.0)
            for c2 in range(c + 1, 8):
                entry = spread(cols[c2][b][c : c + 1, :])
                for g in mult:
                    cols[c2][g] = cols[c2][g] - mult[g] * entry
            row = spread(z[c : c + 1, :])
            if c < 7:
                z = z - mult[b] * row
            for g in range(b + 1, groups):
                w[g] = w[g] - mult[g] * row
        w[b] = jnp.where(lane < j0 + 8, z, 0.0) * lax.rsqrt(pivots)
    return jnp.concatenate(w, axis=0).T


def pack_kernel(modes, mass, pattern, out, sem):
    own, nzb = pattern.shape
    width = out.shape[1]
    held = modes.shape[0]
    first = pltpu.make_async_copy(modes, out.at[pl.ds(0, held)], sem.at[0])
    first.start()
    left = jnp.concatenate([mass[:, i * width : (i + 1) * width] for i in range(own)], axis=0)
    pieces = []
    for _ in range(3):
        pieces.append(left.astype(BF16).astype(F32))
        left = left - pieces[-1]
    pieces.append(jnp.concatenate([pattern[...].astype(F32), jnp.zeros((own, width - nzb), F32)], axis=1))
    used = 4 * own
    lines = out.shape[0] - held
    if lines > used:
        pieces.append(jnp.zeros((lines - used, width), F32))
    out[held:, :] = jnp.concatenate(pieces, axis=0).astype(BF16)
    first.wait()


def gate_kernel(*refs):
    del refs


def filter_kernel(
    nranks, own, nzb, low, high, k0, k1, k2, k3, a0, a1, a2, a3, phi_out, theta_out, rs_out,
    stiff, ya, yb, scale, small, codes, pat, ksem, ysem, ssem, psem,
):
    bs = stiff.shape[1]
    nb = own * nranks
    blk = nzb * bs
    held = own * bs
    lines = small.shape[0] // nranks
    me = lax.axis_index("split")
    cut = own * blk
    copies = []
    for t, ref in enumerate((a0, a1, a2, a3)):
        rank = me ^ t
        copies.append(
            pltpu.make_async_copy(
                ref.at[pl.ds(held, lines)],
                small.at[pl.ds(pl.multiple_of(rank * lines, lines), lines)],
                ssem.at[t],
            )
        )
        copies.append(
            pltpu.make_async_copy(
                ref.at[pl.ds(0, held)],
                ya.at[pl.ds(pl.multiple_of(rank * held, held), held)],
                ysem.at[t],
            )
        )
    parts, kcopies = [], []
    for t, ref in enumerate((k0, k1, k2, k3)):
        parts.append((me ^ t) * own)
        dst = stiff.at[pl.ds(pl.multiple_of(parts[-1] * blk, blk), cut)]
        kcopies.append(pltpu.make_async_copy(ref, dst, ksem.at[t]))
    for c in copies + kcopies:
        c.start()
    for c in copies[::2]:
        c.wait()
    mass = []
    for r in range(nranks):
        rows = small[r * lines : (r + 1) * lines, :].astype(F32)
        codes[r * own : (r + 1) * own, :] = rows[3 * own : 4 * own, :].astype(jnp.int32)
        whole = rows[:own] + rows[own : 2 * own] + rows[2 * own : 3 * own]
        mass += [whole[i : i + 1, :] for i in range(own)]
    down = pltpu.make_async_copy(codes, pat, psem.at[0])
    down.start()
    centre = (high[0] + low[0]) / 2.0
    half = (high[0] - low[0]) / 2.0
    for i in range(nb):
        row = jnp.broadcast_to(mass[i], (bs, bs)).T
        scale[i * bs : (i + 1) * bs, :] = 1.0 / (row * half)
    shift = jnp.full((1, 1), centre, F32) / half
    down.wait()
    for c in copies[1::2]:
        c.wait()

    def image(i, src):
        left = jnp.concatenate([stiff[rows_of(i * nzb + k), :] for k in range(nzb)], axis=1)
        right = jnp.concatenate(
            [src[rows_of(pat[i, k]), :] for k in range(nzb)], axis=0
        )
        return jnp.dot(left, right, preferred_element_type=F32)

    def rows_of(i):
        return pl.ds(i * bs if isinstance(i, int) else pl.multiple_of(i * bs, bs), bs)

    def first(i):
        at = rows_of(i)
        yb[at, :] = (image(i, ya) * scale[at, :] - shift * ya[at, :].astype(F32)).astype(BF16)

    def later(i, src, dst):
        at = rows_of(i)
        dst[at, :] = (
            2.0 * (image(i, src) * scale[at, :] - shift * src[at, :].astype(F32)) - dst[at, :].astype(F32)
        ).astype(BF16)

    def sweep(body):
        for i in range(nb):
            body(i)

    def finish():
        src, dst = yb, ya
        for _ in range(DEG - 1):
            sweep(lambda i, src=src, dst=dst: later(i, src, dst))
            src, dst = dst, src
        cur = src
        gram = jnp.zeros((bs, bs), F32)
        for i in range(nb):
            blk = cur[i * bs : (i + 1) * bs, :]
            row = jnp.broadcast_to(mass[i], (bs, bs)).T
            hi, lo = split2(blk.astype(F32) * row)
            both = lax.dot_general(
                blk, jnp.concatenate([hi, lo], axis=1), (((0,), (0,)), ((), ())), preferred_element_type=F32
            )
            gram = gram + both[:, :bs] + both[:, bs:]
        hi, lo = split2(inverse_factor(gram))
        weights = jnp.concatenate([hi, lo], axis=0)
        for i in range(nb):
            blk = cur[i * bs : (i + 1) * bs, :]
            ya[i * bs : (i + 1) * bs, :] = jnp.dot(
                jnp.concatenate([blk, blk], axis=1), weights, preferred_element_type=F32
            ).astype(BF16)

    @pl.loop(0, ITERS)
    def _(it):
        for t, base in enumerate(parts):

            @pl.when(it == 0)
            def _(t=t):
                kcopies[t].wait()

            for r in range(own):
                first(base + r)
        finish()

    theta = jnp.zeros((8, theta_out.shape[1]), F32)
    for i in range(nb):
        at = rows_of(i)
        prod = ya[at, :].astype(F32) * image(i, ya)
        theta = theta + jnp.sum(prod.reshape(-1, 8, prod.shape[1]), axis=0)
    theta = jnp.sum(theta, axis=0, keepdims=True)
    theta_out[...] = theta
    rs_out[...] = jnp.broadcast_to(lax.rsqrt(theta), rs_out.shape)
    phi_out[...] = ya[...]


def product_kernel(phi, rs, c0, c2, out, held, sem):
    me = lax.axis_index("split")
    njs, bs, cols = c0.shape
    copies = []
    for t, ref in enumerate((c0, c2)):
        copies.append(pltpu.make_async_copy(ref, held.at[t], sem.at[t]))
        copies[-1].start()
    prods = None
    for t, c in enumerate(copies):
        c.wait()
        at = pl.multiple_of((me ^ (2 * t)) * cols, cols)
        part = jnp.dot(held[t].reshape(njs * bs, cols), phi[pl.ds(at, cols), :], preferred_element_type=F32)
        prods = part if prods is None else prods + part
    out[...] = (prods * rs[0:1, :]).astype(BF16).reshape(out.shape)


def face_kernel(nranks, nsub, links, slots, mine, other, keep, send, dense):
    me = lax.axis_index("split")
    faces, share, _ = dense.shape
    first = lax.axis_index("sub") * (faces // nsub)
    dense[...] = jnp.zeros_like(dense)
    for j in range(mine.shape[0]):
        hi, lo = split2(mine[j].astype(F32) + other[j].astype(F32))
        left = jnp.concatenate([hi, lo, hi], axis=1)
        right = jnp.concatenate([hi, hi, lo], axis=1)
        rows = left[:share]
        for r in range(1, nranks):
            rows = jnp.where(me == r, left[share * r : share * (r + 1)], rows)
        dense[slots[links[0, j]] ^ first] = lax.dot_general(
            rows, right, (((1,), (1,)), ((), ())), preferred_element_type=F32
        )
    half = faces // 2
    keep[...] = dense[:half]
    send[...] = dense[half:].astype(BF16)


def shards(stiffness, pattern, mass, start_modes, cut_low, cut_high, coupling, incidence, slot_of):
    stiff = stiffness[0]
    own, nzb, bs, _ = stiff.shape
    modes = start_modes.shape[-1]
    nranks = lax.axis_size("split")
    nsub = lax.axis_size("sub")
    nb = own * nranks
    faces = slot_of.shape[0]
    assert nranks == 4 and nsub & (nsub - 1) == 0

    def swap(x, bits, axis="split", n=nranks):
        return lax.ppermute(x, axis, [(i, i ^ bits) for i in range(n)])

    smem = pl.BlockSpec(memory_space=pltpu.SMEM)
    vmem = pl.BlockSpec(memory_space=pltpu.VMEM)
    hbm = pl.BlockSpec(memory_space=pltpu.HBM)
    blocks = stiff.reshape(-1, bs)
    lines = -(-4 * own // 16) * 16
    a_0 = pl.pallas_call(
        pack_kernel,
        out_shape=jax.ShapeDtypeStruct((own * bs + lines, modes), BF16),
        in_specs=[hbm, vmem, vmem],
        out_specs=vmem,
        scratch_shapes=[pltpu.SemaphoreType.DMA((1,))],
        compiler_params=pltpu.CompilerParams(vmem_limit_bytes=GATE_VMEM),
        name="pack",
    )(start_modes[0], mass, pattern[0])
    k_2 = swap(blocks, 2)
    k_1 = swap(blocks, 1)
    a_2 = swap(a_0, 2)
    a_1 = swap(a_0, 1)
    a_3 = swap(a_2, 1)
    k_2 = pl.pallas_call(
        gate_kernel,
        out_shape=jax.ShapeDtypeStruct(k_2.shape, k_2.dtype),
        in_specs=[hbm] * 2,
        out_specs=hbm,
        input_output_aliases={0: 0},
        compiler_params=pltpu.CompilerParams(vmem_limit_bytes=GATE_VMEM),
        name="gate",
    )(k_2, a_2)
    k_3 = swap(k_2, 1)
    c_2 = swap(coupling[0], 2)

    phi, theta, rs = pl.pallas_call(
        functools.partial(filter_kernel, nranks, own, nzb),
        out_shape=(
            jax.ShapeDtypeStruct((nb * bs, modes), BF16),
            jax.ShapeDtypeStruct((1, modes), F32),
            jax.ShapeDtypeStruct((8, modes), F32),
        ),
        in_specs=[smem, smem] + [hbm] * 8,
        out_specs=(vmem, vmem, vmem),
        scratch_shapes=[
            pltpu.VMEM((nb * nzb * bs, bs), BF16),
            pltpu.VMEM((nb * bs, modes), BF16),
            pltpu.VMEM((nb * bs, modes), BF16),
            pltpu.VMEM((nb * bs, modes), F32),
            pltpu.VMEM((nranks * lines, modes), BF16),
            pltpu.VMEM((nb, modes), jnp.int32),
            pltpu.SMEM((nb, modes), jnp.int32),
            pltpu.SemaphoreType.DMA((4,)),
            pltpu.SemaphoreType.DMA((4,)),
            pltpu.SemaphoreType.DMA((4,)),
            pltpu.SemaphoreType.DMA((1,)),
        ],
        compiler_params=pltpu.CompilerParams(vmem_limit_bytes=FILTER_VMEM),
        cost_estimate=pl.CostEstimate(flops=30_000_000_000, bytes_accessed=8 << 20, transcendentals=0),
        name="filter",
    )(cut_low, cut_high, blocks, k_1, k_2, k_3, a_0, a_1, a_2, a_3)

    share = bs // nranks
    nif, _, cols = coupling.shape[1:]
    prods = pl.pallas_call(
        product_kernel,
        out_shape=jax.ShapeDtypeStruct((nif, bs, modes), BF16),
        in_specs=[vmem, vmem, hbm, hbm],
        out_specs=vmem,
        scratch_shapes=[pltpu.VMEM((2, nif, bs, cols), BF16), pltpu.SemaphoreType.DMA((2,))],
        compiler_params=pltpu.CompilerParams(vmem_limit_bytes=16 << 20),
        name="products",
    )(phi, rs, coupling[0], c_2)
    total, send = pl.pallas_call(
        functools.partial(face_kernel, nranks, nsub),
        out_shape=(
            jax.ShapeDtypeStruct((faces // 2, share, bs), F32),
            jax.ShapeDtypeStruct((faces // 2, share, bs), BF16),
        ),
        in_specs=[smem, smem, vmem, vmem],
        out_specs=(vmem, vmem),
        scratch_shapes=[pltpu.VMEM((faces, share, bs), F32)],
        compiler_params=pltpu.CompilerParams(vmem_limit_bytes=16 << 20),
        name="faces",
    )(incidence, slot_of, prods, swap(prods, 1))
    width = nsub // 2
    while True:
        total = total + swap(send, width, "sub", nsub).astype(F32)
        width //= 2
        if not width:
            break
        at = total.shape[0] // 2
        total, send = total[:at], total[at:].astype(BF16)
    return (total, theta)


def solution(mesh):
    placed = (
        P("sub", "split", None, None, None),
        P("sub", "split", None),
        P("sub", "split"),
        P("sub", "split", None),
        P("sub"),
        P("sub"),
        P("sub", None, None, "split"),
        P("sub", None),
        P(),
    )
    return jax.shard_map(
        shards,
        mesh=mesh,
        in_specs=placed,
        out_specs=(P("sub", "split", None), P("sub", None)),
        check_vma=False,
    )
```

```python
import functools

import jax
import jax.numpy as jnp
from jax import lax
from jax.experimental import pallas as pl
from jax.experimental.pallas import tpu as pltpu
from jax.sharding import PartitionSpec as P

DEG = 4
ITERS = 2
F32 = jnp.float32
BF16 = jnp.bfloat16
GATE_VMEM = 24 << 20
FILTER_VMEM = 24 << 20


def split2(x):
    hi = x.astype(BF16)
    return hi, (x - hi.astype(F32)).astype(BF16)


def split3(x):
    hi = x.astype(BF16)
    mid, lo = split2(x - hi.astype(F32))
    return hi, mid, lo


def stack(parts):
    return jnp.concatenate([p.astype(F32) for p in parts], axis=0).astype(BF16)


def inverse_factor(gram, between, near=3):
    n = gram.shape[0]
    lane = lax.broadcasted_iota(jnp.int32, (8, n), 1)
    sub = lax.broadcasted_iota(jnp.int32, (8, n), 0)
    groups = n // 8
    w = [gram[8 * g : 8 * g + 8, :] for g in range(groups)]

    def spread(x):
        return jnp.broadcast_to(x, (8, n))

    ahead = [spread(w[0][:, c : c + 1]) for c in range(8)]
    for b in range(groups):
        j0 = 8 * b
        top = min(groups, b + near + 1)
        inside = (lane >= j0) & (lane < j0 + 8)
        cols = [{b: ahead[c]} for c in range(8)]
        for g in range(b + 1, top):
            for c in range(8):
                cols[c][g] = spread(w[g][:, j0 + c : j0 + c + 1])
        ahead = []
        if b + 1 < groups:
            ahead = [spread(w[b + 1][:, j0 + 8 + c : j0 + 9 + c]) for c in range(8)]
        z = jnp.where(inside, jnp.where(lane == sub + j0, 1.0, 0.0), w[b])
        for g in range(b + 1, groups):
            w[g] = jnp.where(inside, 0.0, w[g])
        pivots = jnp.ones((8, n), F32)
        inverses = jnp.ones((8, n), F32)
        for c in range(8):
            pivot = spread(cols[c][b][c : c + 1, :])
            inv = 1.0 / pivot
            pivots = jnp.where(sub == c, pivot, pivots)
            inverses = jnp.where(sub == c, inv, inverses)
            mult = {g: cols[c][g] * inv for g in range(b + 1, top)}
            if c < 7:
                mult[b] = jnp.where(sub > c, cols[c][b] * inv, 0.0)
            for c2 in range(c + 1, 8):
                entry = spread(cols[c2][b][c : c + 1, :])
                for g in mult:
                    cols[c2][g] = cols[c2][g] - mult[g] * entry
            for c2 in range(len(ahead)):
                ahead[c2] = ahead[c2] - mult[b + 1] * spread(cols[c][b + 1][c2 : c2 + 1, :])
            row = spread(z[c : c + 1, :])
            if c < 7:
                z = z - mult[b] * row
            for g in range(b + 1, top):
                w[g] = w[g] - mult[g] * row
        if top < groups:
            a1, a2, a3 = split3(z * inverses)
            b1, b2, b3 = split3(z)
            update = lax.dot_general(
                stack((a1, a1, a2, a2, a1, a3)),
                stack((b1, b2, b1, b2, b3, b1)),
                (((0,), (0,)), ((), ())),
                preferred_element_type=F32,
            )
            for g in range(top, groups):
                w[g] = w[g] - update[8 * g : 8 * g + 8, :]
        w[b] = jnp.where(lane < j0 + 8, z, 0.0) * lax.rsqrt(pivots)
        between(b)
    return jnp.concatenate(w, axis=0).T


def pack_kernel(modes, mass, pattern, out, sem):
    own, nzb = pattern.shape
    width = out.shape[1]
    held = modes.shape[0]
    first = pltpu.make_async_copy(modes, out.at[pl.ds(0, held)], sem.at[0])
    first.start()
    left = jnp.concatenate([mass[:, i * width : (i + 1) * width] for i in range(own)], axis=0)
    pieces = []
    for _ in range(3):
        pieces.append(left.astype(BF16).astype(F32))
        left = left - pieces[-1]
    pieces.append(jnp.concatenate([pattern[...].astype(F32), jnp.zeros((own, width - nzb), F32)], axis=1))
    used = 4 * own
    lines = out.shape[0] - held
    if lines > used:
        pieces.append(jnp.zeros((lines - used, width), F32))
    out[held:, :] = jnp.concatenate(pieces, axis=0).astype(BF16)
    first.wait()


def gate_kernel(*refs):
    del refs


def filter_kernel(
    nranks, own, nzb, low, high, k0, k1, k2, k3, a0, a1, a2, a3, phi_out, theta_out, rs_out,
    ya, yb, zs, scale, codes, pat, psem,
):
    bs = k0.shape[1]
    nb = own * nranks
    held = own * bs
    me = lax.axis_index("split")
    kept = (k0, k1, k2, k3)

    def rows_of(i):
        return pl.ds(i * bs if isinstance(i, int) else pl.multiple_of(i * bs, bs), bs)

    mass = [None] * nb
    lines = a0.shape[0] - held
    smalls = [ref[held:, :].astype(F32) for ref in (a0, a1, a2, a3)]
    for r in range(nranks):
        rows = smalls[0]
        for t in range(1, nranks):
            rows = jnp.where((me ^ t) == r, smalls[t], rows)
        rows = jnp.where(me == r, smalls[0], rows)
        codes[r * own : (r + 1) * own, :] = rows[3 * own : 4 * own, :].astype(jnp.int32)
        whole = rows[:own] + rows[own : 2 * own] + rows[2 * own : 3 * own]
        for i in range(own):
            mass[r * own + i] = whole[i : i + 1, :]
    down = pltpu.make_async_copy(codes, pat, psem.at[0])
    down.start()
    for t, ref in enumerate((a0, a1, a2, a3)):
        ya[pl.ds(pl.multiple_of((me ^ t) * held, held), held), :] = ref[:held, :]
    centre = (high[0] + low[0]) / 2.0
    half = (high[0] - low[0]) / 2.0
    for i in range(nb):
        row = jnp.broadcast_to(mass[i], (bs, bs)).T
        scale[i * bs : (i + 1) * bs, :] = 1.0 / (row * half)
    shift = jnp.full((1, 1), centre, F32) / half
    down.wait()

    def order():
        for t in range(nranks):
            for r in range(own):
                yield t, r, (me ^ t) * own + r

    def image(t, r, i, src):
        left = jnp.concatenate([kept[t][rows_of(r * nzb + k), :] for k in range(nzb)], axis=1)
        right = jnp.concatenate([src[rows_of(pat[i, k]), :] for k in range(nzb)], axis=0)
        return jnp.dot(left, right, preferred_element_type=F32)

    for t, r, i in order():
        at = rows_of(i)
        yb[at, :] = (image(t, r, i, ya) * scale[at, :] - shift * ya[at, :].astype(F32)).astype(BF16)

    @pl.loop(0, ITERS)
    def _(it):
        src, dst = yb, ya
        for _ in range(DEG - 1):
            for t, r, i in order():
                at = rows_of(i)
                dst[at, :] = (
                    2.0 * (image(t, r, i, src) * scale[at, :] - shift * src[at, :].astype(F32))
                    - dst[at, :].astype(F32)
                ).astype(BF16)
            src, dst = dst, src
        cur = src
        gram = jnp.zeros((bs, bs), F32)
        for i in range(nb):
            blk = cur[rows_of(i), :]
            row = jnp.broadcast_to(mass[i], (bs, bs)).T
            hi, lo = split2(blk.astype(F32) * row)
            both = lax.dot_general(
                blk, jnp.concatenate([hi, lo], axis=1), (((0,), (0,)), ((), ())), preferred_element_type=F32
            )
            gram = gram + both[:, :bs] + both[:, bs:]
        todo = list(order())

        def between(b):
            for t, r, i in todo[nb * b // groups : nb * (b + 1) // groups]:
                hi, lo = split2(image(t, r, i, cur))
                zs[rows_of(i), :bs] = hi
                zs[rows_of(i), bs:] = lo

        groups = bs // 8
        hi, lo = split2(inverse_factor(gram, between))
        twice = jnp.concatenate([hi, lo], axis=0)
        thrice = jnp.concatenate([hi, hi, lo], axis=0)
        theta = jnp.zeros((8, bs), F32)
        for i in range(nb):
            at = rows_of(i)
            blk = cur[at, :]
            phi = jnp.dot(jnp.concatenate([blk, blk], axis=1), twice, preferred_element_type=F32).astype(BF16)
            both = zs[at, :]
            img = jnp.dot(
                jnp.concatenate([both, both[:, :bs]], axis=1), thrice, preferred_element_type=F32
            )
            ya[at, :] = phi
            phi = phi.astype(F32)
            yb[at, :] = (img * scale[at, :] - shift * phi).astype(BF16)
            theta = theta + jnp.sum((phi * img).reshape(-1, 8, bs), axis=0)
        theta = jnp.sum(theta, axis=0, keepdims=True)
        theta_out[...] = theta
        rs_out[...] = jnp.broadcast_to(lax.rsqrt(theta), rs_out.shape)

    phi_out[...] = ya[...]


def product_kernel(phi, rs, c0, c2, out, held, sem):
    me = lax.axis_index("split")
    njs, bs, cols = c0.shape
    copies = []
    for t, ref in enumerate((c0, c2)):
        copies.append(pltpu.make_async_copy(ref, held.at[t], sem.at[t]))
        copies[-1].start()
    prods = None
    for t, c in enumerate(copies):
        c.wait()
        at = pl.multiple_of((me ^ (2 * t)) * cols, cols)
        part = jnp.dot(held[t].reshape(njs * bs, cols), phi[pl.ds(at, cols), :], preferred_element_type=F32)
        prods = part if prods is None else prods + part
    out[...] = (prods * rs[0:1, :]).astype(BF16).reshape(out.shape)


def face_kernel(nranks, nsub, links, slots, mine, other, keep, send, dense):
    me = lax.axis_index("split")
    faces, share, _ = dense.shape
    first = lax.axis_index("sub") * (faces // nsub)
    dense[...] = jnp.zeros_like(dense)
    for j in range(mine.shape[0]):
        hi, lo = split2(mine[j].astype(F32) + other[j].astype(F32))
        left = jnp.concatenate([hi, lo, hi], axis=1)
        right = jnp.concatenate([hi, hi, lo], axis=1)
        rows = left[:share]
        for r in range(1, nranks):
            rows = jnp.where(me == r, left[share * r : share * (r + 1)], rows)
        dense[slots[links[0, j]] ^ first] = lax.dot_general(
            rows, right, (((1,), (1,)), ((), ())), preferred_element_type=F32
        )
    half = faces // 2
    keep[...] = dense[:half]
    send[...] = dense[half:].astype(BF16)


def shards(stiffness, pattern, mass, start_modes, cut_low, cut_high, coupling, incidence, slot_of):
    stiff = stiffness[0]
    own, nzb, bs, _ = stiff.shape
    modes = start_modes.shape[-1]
    nranks = lax.axis_size("split")
    nsub = lax.axis_size("sub")
    nb = own * nranks
    faces = slot_of.shape[0]
    assert nranks == 4 and nsub & (nsub - 1) == 0

    def swap(x, bits, axis="split", n=nranks):
        return lax.ppermute(x, axis, [(i, i ^ bits) for i in range(n)])

    smem = pl.BlockSpec(memory_space=pltpu.SMEM)
    vmem = pl.BlockSpec(memory_space=pltpu.VMEM)
    hbm = pl.BlockSpec(memory_space=pltpu.HBM)
    blocks = stiff.reshape(-1, bs)
    lines = -(-4 * own // 16) * 16
    a_0 = pl.pallas_call(
        pack_kernel,
        out_shape=jax.ShapeDtypeStruct((own * bs + lines, modes), BF16),
        in_specs=[hbm, vmem, vmem],
        out_specs=vmem,
        scratch_shapes=[pltpu.SemaphoreType.DMA((1,))],
        compiler_params=pltpu.CompilerParams(vmem_limit_bytes=GATE_VMEM),
        name="pack",
    )(start_modes[0], mass, pattern[0])
    k_2 = swap(blocks, 2)
    k_1 = swap(blocks, 1)
    a_2 = swap(a_0, 2)
    a_1 = swap(a_0, 1)
    a_3 = swap(a_2, 1)
    k_2 = pl.pallas_call(
        gate_kernel,
        out_shape=jax.ShapeDtypeStruct(k_2.shape, k_2.dtype),
        in_specs=[hbm] * 2,
        out_specs=hbm,
        input_output_aliases={0: 0},
        compiler_params=pltpu.CompilerParams(vmem_limit_bytes=GATE_VMEM),
        name="gate",
    )(k_2, a_2)
    k_3 = swap(k_2, 1)
    c_2 = swap(coupling[0], 2)

    phi, theta, rs = pl.pallas_call(
        functools.partial(filter_kernel, nranks, own, nzb),
        out_shape=(
            jax.ShapeDtypeStruct((nb * bs, modes), BF16),
            jax.ShapeDtypeStruct((1, modes), F32),
            jax.ShapeDtypeStruct((8, modes), F32),
        ),
        in_specs=[smem, smem] + [vmem] * 8,
        out_specs=(vmem, vmem, vmem),
        scratch_shapes=[
            pltpu.VMEM((nb * bs, modes), BF16),
            pltpu.VMEM((nb * bs, modes), BF16),
            pltpu.VMEM((nb * bs, 2 * modes), BF16),
            pltpu.VMEM((nb * bs, modes), F32),
            pltpu.VMEM((nb, modes), jnp.int32),
            pltpu.SMEM((nb, modes), jnp.int32),
            pltpu.SemaphoreType.DMA((1,)),
        ],
        compiler_params=pltpu.CompilerParams(vmem_limit_bytes=FILTER_VMEM),
        cost_estimate=pl.CostEstimate(flops=30_000_000_000, bytes_accessed=8 << 20, transcendentals=0),
        name="filter",
    )(cut_low, cut_high, blocks, k_1, k_2, k_3, a_0, a_1, a_2, a_3)

    share = bs // nranks
    nif, _, cols = coupling.shape[1:]
    prods = pl.pallas_call(
        product_kernel,
        out_shape=jax.ShapeDtypeStruct((nif, bs, modes), BF16),
        in_specs=[vmem, vmem, hbm, hbm],
        out_specs=vmem,
        scratch_shapes=[pltpu.VMEM((2, nif, bs, cols), BF16), pltpu.SemaphoreType.DMA((2,))],
        compiler_params=pltpu.CompilerParams(vmem_limit_bytes=16 << 20),
        name="products",
    )(phi, rs, coupling[0], c_2)
    total, send = pl.pallas_call(
        functools.partial(face_kernel, nranks, nsub),
        out_shape=(
            jax.ShapeDtypeStruct((faces // 2, share, bs), F32),
            jax.ShapeDtypeStruct((faces // 2, share, bs), BF16),
        ),
        in_specs=[smem, smem, vmem, vmem],
        out_specs=(vmem, vmem),
        scratch_shapes=[pltpu.VMEM((faces, share, bs), F32)],
        compiler_params=pltpu.CompilerParams(vmem_limit_bytes=16 << 20),
        name="faces",
    )(incidence, slot_of, prods, swap(prods, 1))
    width = nsub // 2
    while True:
        total = total + swap(send, width, "sub", nsub).astype(F32)
        width //= 2
        if not width:
            break
        at = total.shape[0] // 2
        total, send = total[:at], total[at:].astype(BF16)
    return (total, theta)


def solution(mesh):
    placed = (
        P("sub", "split", None, None, None),
        P("sub", "split", None),
        P("sub", "split"),
        P("sub", "split", None),
        P("sub"),
        P("sub"),
        P("sub", None, None, "split"),
        P("sub", None),
        P(),
    )
    return jax.shard_map(
        shards,
        mesh=mesh,
        in_specs=placed,
        out_specs=(P("sub", "split", None), P("sub", None)),
        check_vma=False,
    )
```

```python
import functools

import jax
import jax.numpy as jnp
from jax import lax
from jax.experimental import pallas as pl
from jax.experimental.pallas import tpu as pltpu
from jax.sharding import PartitionSpec as P

DEG = 4
ITERS = 2
F32 = jnp.float32
BF16 = jnp.bfloat16
XFLOPS = 5_000_000_000
FFLOPS = 1_000_000_000
SPLIT = 2
GATE_VMEM = 24 << 20
FILTER_VMEM = 24 << 20


def split2(x):
    hi = x.astype(BF16)
    return hi, (x - hi.astype(F32)).astype(BF16)


def split3(x):
    hi = x.astype(BF16)
    mid, lo = split2(x - hi.astype(F32))
    return hi, mid, lo


def stack(parts):
    return jnp.concatenate([p.astype(F32) for p in parts], axis=0).astype(BF16)


def inverse_factor(gram, between, near=3):
    n = gram.shape[0]
    lane = lax.broadcasted_iota(jnp.int32, (8, n), 1)
    sub = lax.broadcasted_iota(jnp.int32, (8, n), 0)
    groups = n // 8
    w = [gram[8 * g : 8 * g + 8, :] for g in range(groups)]

    def spread(x):
        return jnp.broadcast_to(x, (8, n))

    ahead = [spread(w[0][:, c : c + 1]) for c in range(8)]
    for b in range(groups):
        j0 = 8 * b
        top = min(groups, b + near + 1)
        inside = (lane >= j0) & (lane < j0 + 8)
        cols = [{b: ahead[c]} for c in range(8)]
        for g in range(b + 1, top):
            for c in range(8):
                cols[c][g] = spread(w[g][:, j0 + c : j0 + c + 1])
        ahead = []
        if b + 1 < groups:
            ahead = [spread(w[b + 1][:, j0 + 8 + c : j0 + 9 + c]) for c in range(8)]
        z = jnp.where(inside, jnp.where(lane == sub + j0, 1.0, 0.0), w[b])
        for g in range(b + 1, groups):
            w[g] = jnp.where(inside, 0.0, w[g])
        pivots = jnp.ones((8, n), F32)
        inverses = jnp.ones((8, n), F32)
        for c in range(8):
            pivot = spread(cols[c][b][c : c + 1, :])
            inv = 1.0 / pivot
            pivots = jnp.where(sub == c, pivot, pivots)
            inverses = jnp.where(sub == c, inv, inverses)
            mult = {g: cols[c][g] * inv for g in range(b + 1, top)}
            if c < 7:
                mult[b] = jnp.where(sub > c, cols[c][b] * inv, 0.0)
            for c2 in range(c + 1, 8):
                entry = spread(cols[c2][b][c : c + 1, :])
                for g in mult:
                    cols[c2][g] = cols[c2][g] - mult[g] * entry
            for c2 in range(len(ahead)):
                ahead[c2] = ahead[c2] - mult[b + 1] * spread(cols[c][b + 1][c2 : c2 + 1, :])
            row = spread(z[c : c + 1, :])
            if c < 7:
                z = z - mult[b] * row
            for g in range(b + 1, top):
                w[g] = w[g] - mult[g] * row
        if top < groups:
            a1, a2, a3 = split3(z * inverses)
            b1, b2, b3 = split3(z)
            update = lax.dot_general(
                stack((a1, a1, a2, a2, a1, a3)),
                stack((b1, b2, b1, b2, b3, b1)),
                (((0,), (0,)), ((), ())),
                preferred_element_type=F32,
            )
            for g in range(top, groups):
                w[g] = w[g] - update[8 * g : 8 * g + 8, :]
        w[b] = jnp.where(lane < j0 + 8, z, 0.0) * lax.rsqrt(pivots)
        between(b)
    return jnp.concatenate(w, axis=0).T


def pack_kernel(modes, mass, pattern, blocks, out, sem):
    del blocks
    own, nzb = pattern.shape
    width = out.shape[1]
    held = modes.shape[0]
    first = pltpu.make_async_copy(modes, out.at[pl.ds(0, held)], sem.at[0])
    first.start()
    left = jnp.concatenate([mass[:, i * width : (i + 1) * width] for i in range(own)], axis=0)
    pieces = []
    for _ in range(3):
        pieces.append(left.astype(BF16).astype(F32))
        left = left - pieces[-1]
    pieces.append(jnp.concatenate([pattern[...].astype(F32), jnp.zeros((own, width - nzb), F32)], axis=1))
    used = 4 * own
    lines = out.shape[0] - held
    if lines > used:
        pieces.append(jnp.zeros((lines - used, width), F32))
    out[held:, :] = jnp.concatenate(pieces, axis=0).astype(BF16)
    first.wait()


def gate_kernel(*refs):
    del refs


def filter_kernel(
    nranks, own, nzb, low, high, k0, k1, k2, *refs,
):
    k3, refs = refs[:SPLIT], refs[SPLIT:]
    (
        a0, a1, a2, a3, phi_out, theta_out, rs_out,
        ya, yb, zs, scale, heavy, codes, pat, mine, psem, ksem,
    ) = refs
    fetch = pltpu.make_async_copy(k0, mine, ksem.at[0])
    fetch.start()
    bs = k0.shape[1]
    nb = own * nranks
    held = own * bs
    me = lax.axis_index("split")
    kept = (mine, k1, k2)

    def rows_of(i):
        return pl.ds(i * bs if isinstance(i, int) else pl.multiple_of(i * bs, bs), bs)

    mass = [None] * nb
    lines = a0.shape[0] - held
    smalls = [ref[held:, :].astype(F32) for ref in (a0, a1, a2, a3)]
    for r in range(nranks):
        rows = smalls[0]
        for t in range(1, nranks):
            rows = jnp.where((me ^ t) == r, smalls[t], rows)
        rows = jnp.where(me == r, smalls[0], rows)
        codes[r * own : (r + 1) * own, :] = rows[3 * own : 4 * own, :].astype(jnp.int32)
        whole = rows[:own] + rows[own : 2 * own] + rows[2 * own : 3 * own]
        for i in range(own):
            mass[r * own + i] = whole[i : i + 1, :]
    down = pltpu.make_async_copy(codes, pat, psem.at[0])
    down.start()
    for t, ref in enumerate((a0, a1, a2, a3)):
        ya[pl.ds(pl.multiple_of((me ^ t) * held, held), held), :] = ref[:held, :]
    centre = (high[0] + low[0]) / 2.0
    half = (high[0] - low[0]) / 2.0
    for i in range(nb):
        row = jnp.broadcast_to(mass[i], (bs, bs)).T
        heavy[i * bs : (i + 1) * bs, :] = row
        scale[i * bs : (i + 1) * bs, :] = 1.0 / (row * half)
    shift = jnp.full((1, 1), centre, F32) / half
    down.wait()

    def order():
        for t in range(nranks):
            for r in range(own):
                yield t, r, (me ^ t) * own + r

    def image(t, r, i, src):
        if t < 3:
            left = [kept[t][rows_of(r * nzb + k), :] for k in range(nzb)]
        else:
            per = own // SPLIT
            left = [k3[r // per][rows_of(r % per * nzb + k), :] for k in range(nzb)]
        left = jnp.concatenate(left, axis=1)
        right = jnp.concatenate([src[rows_of(pat[i, k]), :] for k in range(nzb)], axis=0)
        return jnp.dot(left, right, preferred_element_type=F32)

    for t, r, i in sorted(order(), key=lambda x: x[0] == 0):
        if (t, r) == (0, 0):
            fetch.wait()
        at = rows_of(i)
        yb[at, :] = (image(t, r, i, ya) * scale[at, :] - shift * ya[at, :].astype(F32)).astype(BF16)

    @pl.loop(0, ITERS)
    def _(it):
        src, dst = yb, ya
        for _ in range(DEG - 1):
            for t, r, i in order():
                at = rows_of(i)
                dst[at, :] = (
                    2.0 * (image(t, r, i, src) * scale[at, :] - shift * src[at, :].astype(F32))
                    - dst[at, :].astype(F32)
                ).astype(BF16)
            src, dst = dst, src
        cur = src
        gram = jnp.zeros((bs, bs), F32)
        for i in range(nb):
            blk = cur[rows_of(i), :]
            hi, lo = split2(blk.astype(F32) * heavy[rows_of(i), :])
            both = lax.dot_general(
                blk, jnp.concatenate([hi, lo], axis=1), (((0,), (0,)), ((), ())), preferred_element_type=F32
            )
            gram = gram + both[:, :bs] + both[:, bs:]
        todo = list(order())

        def between(b):
            for t, r, i in todo[nb * b // groups : nb * (b + 1) // groups]:
                zs[rows_of(i), :] = image(t, r, i, cur).astype(BF16)

        groups = bs // 8
        hi, lo = split2(inverse_factor(gram, between))
        twice = jnp.concatenate([hi, lo], axis=0)
        theta = jnp.zeros((8, bs), F32)
        for i in range(nb):
            at = rows_of(i)
            blk = cur[at, :]
            phi = jnp.dot(jnp.concatenate([blk, blk], axis=1), twice, preferred_element_type=F32).astype(BF16)
            blk = zs[at, :]
            img = jnp.dot(jnp.concatenate([blk, blk], axis=1), twice, preferred_element_type=F32)
            ya[at, :] = phi
            phi = phi.astype(F32)
            yb[at, :] = (img * scale[at, :] - shift * phi).astype(BF16)
            theta = theta + jnp.sum((phi * img).reshape(-1, 8, bs), axis=0)
        theta = jnp.sum(theta, axis=0, keepdims=True)
        theta_out[...] = theta
        rs_out[...] = jnp.broadcast_to(lax.rsqrt(theta), rs_out.shape)

    phi_out[...] = ya[...]


def product_kernel(phi, rs, c0, c2, out, held, sem):
    me = lax.axis_index("split")
    njs, bs, cols = c0.shape
    copies = []
    for t, ref in enumerate((c0, c2)):
        copies.append(pltpu.make_async_copy(ref, held.at[t], sem.at[t]))
        copies[-1].start()
    prods = None
    for t, c in enumerate(copies):
        c.wait()
        at = pl.multiple_of((me ^ (2 * t)) * cols, cols)
        part = jnp.dot(held[t].reshape(njs * bs, cols), phi[pl.ds(at, cols), :], preferred_element_type=F32)
        prods = part if prods is None else prods + part
    out[...] = (prods * rs[0:1, :]).astype(BF16).reshape(out.shape)


def face_kernel(nranks, nsub, links, slots, mine, other, keep, send, dense):
    me = lax.axis_index("split")
    faces, share, _ = dense.shape
    first = lax.axis_index("sub") * (faces // nsub)
    dense[...] = jnp.zeros_like(dense)
    for j in range(mine.shape[0]):
        hi, lo = split2(mine[j].astype(F32) + other[j].astype(F32))
        left = jnp.concatenate([hi, lo, hi], axis=1)
        right = jnp.concatenate([hi, hi, lo], axis=1)
        rows = left[:share]
        for r in range(1, nranks):
            rows = jnp.where(me == r, left[share * r : share * (r + 1)], rows)
        dense[slots[links[0, j]] ^ first] = lax.dot_general(
            rows, right, (((1,), (1,)), ((), ())), preferred_element_type=F32
        )
    half = faces // 2
    keep[...] = dense[:half]
    send[...] = dense[half:].astype(BF16)


def shards(stiffness, pattern, mass, start_modes, cut_low, cut_high, coupling, incidence, slot_of):
    stiff = stiffness[0]
    own, nzb, bs, _ = stiff.shape
    modes = start_modes.shape[-1]
    nranks = lax.axis_size("split")
    nsub = lax.axis_size("sub")
    nb = own * nranks
    faces = slot_of.shape[0]
    assert nranks == 4 and nsub & (nsub - 1) == 0

    def swap(x, bits, axis="split", n=nranks):
        return lax.ppermute(x, axis, [(i, i ^ bits) for i in range(n)])

    smem = pl.BlockSpec(memory_space=pltpu.SMEM)
    vmem = pl.BlockSpec(memory_space=pltpu.VMEM)
    hbm = pl.BlockSpec(memory_space=pltpu.HBM)
    blocks = stiff.reshape(-1, bs)
    lines = -(-4 * own // 16) * 16
    a_0 = pl.pallas_call(
        pack_kernel,
        out_shape=jax.ShapeDtypeStruct((own * bs + lines, modes), BF16),
        in_specs=[hbm, vmem, vmem, hbm],
        out_specs=vmem,
        scratch_shapes=[pltpu.SemaphoreType.DMA((1,))],
        compiler_params=pltpu.CompilerParams(vmem_limit_bytes=GATE_VMEM),
        name="pack",
    )(start_modes[0], mass, pattern[0], blocks)
    k_2 = swap(blocks, 2)
    k_1 = swap(blocks, 1)
    a_2 = swap(a_0, 2)
    a_1 = swap(a_0, 1)
    a_2 = pl.pallas_call(
        gate_kernel,
        out_shape=jax.ShapeDtypeStruct(a_2.shape, a_2.dtype),
        in_specs=[hbm] * 2,
        out_specs=hbm,
        input_output_aliases={0: 0},
        compiler_params=pltpu.CompilerParams(vmem_limit_bytes=GATE_VMEM),
        name="gate",
    )(a_2, a_1)
    a_3 = swap(a_2, 1)
    a_3 = pl.pallas_call(
        gate_kernel,
        out_shape=jax.ShapeDtypeStruct(a_3.shape, a_3.dtype),
        in_specs=[hbm],
        out_specs=hbm,
        input_output_aliases={0: 0},
        compiler_params=pltpu.CompilerParams(vmem_limit_bytes=GATE_VMEM),
        cost_estimate=pl.CostEstimate(flops=XFLOPS, bytes_accessed=0, transcendentals=0),
        name="gate",
    )(a_3)
    part = k_2.shape[0] // SPLIT
    k_3 = [swap(k_2[i * part : (i + 1) * part], 1) for i in range(SPLIT)]
    c_2 = swap(coupling[0], 2)

    phi, theta, rs = pl.pallas_call(
        functools.partial(filter_kernel, nranks, own, nzb),
        out_shape=(
            jax.ShapeDtypeStruct((nb * bs, modes), BF16),
            jax.ShapeDtypeStruct((1, modes), F32),
            jax.ShapeDtypeStruct((8, modes), F32),
        ),
        in_specs=[smem, smem, hbm] + [vmem] * (6 + SPLIT),
        out_specs=(vmem, vmem, vmem),
        scratch_shapes=[
            pltpu.VMEM((nb * bs, modes), BF16),
            pltpu.VMEM((nb * bs, modes), BF16),
            pltpu.VMEM((nb * bs, modes), BF16),
            pltpu.VMEM((nb * bs, modes), F32),
            pltpu.VMEM((nb * bs, modes), F32),
            pltpu.VMEM((nb, modes), jnp.int32),
            pltpu.SMEM((nb, modes), jnp.int32),
            pltpu.VMEM(blocks.shape, BF16),
            pltpu.SemaphoreType.DMA((1,)),
            pltpu.SemaphoreType.DMA((1,)),
        ],
        compiler_params=pltpu.CompilerParams(vmem_limit_bytes=FILTER_VMEM),
        cost_estimate=pl.CostEstimate(flops=FFLOPS, bytes_accessed=8 << 20, transcendentals=0),
        name="filter",
    )(cut_low, cut_high, blocks, k_1, k_2, *k_3, a_0, a_1, a_2, a_3)

    share = bs // nranks
    nif, _, cols = coupling.shape[1:]
    prods = pl.pallas_call(
        product_kernel,
        out_shape=jax.ShapeDtypeStruct((nif, bs, modes), BF16),
        in_specs=[vmem, vmem, hbm, hbm],
        out_specs=vmem,
        scratch_shapes=[pltpu.VMEM((2, nif, bs, cols), BF16), pltpu.SemaphoreType.DMA((2,))],
        compiler_params=pltpu.CompilerParams(vmem_limit_bytes=16 << 20),
        name="products",
    )(phi, rs, coupling[0], c_2)
    total, send = pl.pallas_call(
        functools.partial(face_kernel, nranks, nsub),
        out_shape=(
            jax.ShapeDtypeStruct((faces // 2, share, bs), F32),
            jax.ShapeDtypeStruct((faces // 2, share, bs), BF16),
        ),
        in_specs=[smem, smem, vmem, vmem],
        out_specs=(vmem, vmem),
        scratch_shapes=[pltpu.VMEM((faces, share, bs), F32)],
        compiler_params=pltpu.CompilerParams(vmem_limit_bytes=16 << 20),
        name="faces",
    )(incidence, slot_of, prods, swap(prods, 1))
    width = nsub // 2
    while True:
        total = total + swap(send, width, "sub", nsub).astype(F32)
        width //= 2
        if not width:
            break
        at = total.shape[0] // 2
        total, send = total[:at], total[at:].astype(BF16)
    return (total, theta)


def solution(mesh):
    placed = (
        P("sub", "split", None, None, None),
        P("sub", "split", None),
        P("sub", "split"),
        P("sub", "split", None),
        P("sub"),
        P("sub"),
        P("sub", None, None, "split"),
        P("sub", None),
        P(),
    )
    return jax.shard_map(
        shards,
        mesh=mesh,
        in_specs=placed,
        out_specs=(P("sub", "split", None), P("sub", None)),
        check_vma=False,
    )
```

```python
import functools

import jax
import jax.numpy as jnp
from jax import lax
from jax.experimental import pallas as pl
from jax.experimental.pallas import tpu as pltpu
from jax.sharding import PartitionSpec as P

DEG = 4
ITERS = 2
F32 = jnp.float32
BF16 = jnp.bfloat16
XFLOPS = 5_000_000_000
FFLOPS = 1_000_000_000
SPLIT = 2
GATE_VMEM = 24 << 20
FILTER_VMEM = 24 << 20


def split2(x):
    hi = x.astype(BF16)
    return hi, (x - hi.astype(F32)).astype(BF16)


def split3(x):
    hi = x.astype(BF16)
    mid, lo = split2(x - hi.astype(F32))
    return hi, mid, lo


def stack(parts):
    return jnp.concatenate([p.astype(F32) for p in parts], axis=0).astype(BF16)


def inverse_factor(gram, between, near=2):
    n = gram.shape[0]
    lane = lax.broadcasted_iota(jnp.int32, (8, n), 1)
    sub = lax.broadcasted_iota(jnp.int32, (8, n), 0)
    groups = n // 8
    w = [gram[8 * g : 8 * g + 8, :] for g in range(groups)]

    def spread(x):
        return jnp.broadcast_to(x, (8, n))

    ahead = [spread(w[0][:, c : c + 1]) for c in range(8)]
    for b in range(groups):
        j0 = 8 * b
        top = min(groups, b + near + 1)
        inside = (lane >= j0) & (lane < j0 + 8)
        cols = [{b: ahead[c]} for c in range(8)]
        for g in range(b + 1, top):
            for c in range(8):
                cols[c][g] = spread(w[g][:, j0 + c : j0 + c + 1])
        ahead = []
        if b + 1 < groups:
            ahead = [spread(w[b + 1][:, j0 + 8 + c : j0 + 9 + c]) for c in range(8)]
        z = jnp.where(inside, jnp.where(lane == sub + j0, 1.0, 0.0), w[b])
        for g in range(b + 1, groups):
            w[g] = jnp.where(inside, 0.0, w[g])
        pivots = jnp.ones((8, n), F32)
        inverses = jnp.ones((8, n), F32)
        for c in range(8):
            pivot = spread(cols[c][b][c : c + 1, :])
            inv = 1.0 / pivot
            pivots = jnp.where(sub == c, pivot, pivots)
            inverses = jnp.where(sub == c, inv, inverses)
            mult = {g: cols[c][g] * inv for g in range(b + 1, top)}
            if c < 7:
                mult[b] = jnp.where(sub > c, cols[c][b] * inv, 0.0)
            for c2 in range(c + 1, 8):
                entry = spread(cols[c2][b][c : c + 1, :])
                for g in mult:
                    cols[c2][g] = cols[c2][g] - mult[g] * entry
            for c2 in range(len(ahead)):
                ahead[c2] = ahead[c2] - mult[b + 1] * spread(cols[c][b + 1][c2 : c2 + 1, :])
            row = spread(z[c : c + 1, :])
            if c < 7:
                z = z - mult[b] * row
            for g in range(b + 1, top):
                w[g] = w[g] - mult[g] * row
        if top < groups:
            a1, a2, a3 = split3(z * inverses)
            b1, b2, b3 = split3(z)
            update = lax.dot_general(
                stack((a1, a1, a2, a2, a1, a3)),
                stack((b1, b2, b1, b2, b3, b1)),
                (((0,), (0,)), ((), ())),
                preferred_element_type=F32,
            )
            for g in range(top, groups):
                w[g] = w[g] - update[8 * g : 8 * g + 8, :]
        w[b] = jnp.where(lane < j0 + 8, z, 0.0) * lax.rsqrt(pivots)
        between(b)
    return jnp.concatenate(w, axis=0).T


def pack_kernel(modes, mass, pattern, blocks, out, sem):
    del blocks
    own, nzb = pattern.shape
    width = out.shape[1]
    held = modes.shape[0]
    first = pltpu.make_async_copy(modes, out.at[pl.ds(0, held)], sem.at[0])
    first.start()
    left = jnp.concatenate([mass[:, i * width : (i + 1) * width] for i in range(own)], axis=0)
    pieces = []
    for _ in range(3):
        pieces.append(left.astype(BF16).astype(F32))
        left = left - pieces[-1]
    pieces.append(jnp.concatenate([pattern[...].astype(F32), jnp.zeros((own, width - nzb), F32)], axis=1))
    used = 4 * own
    lines = out.shape[0] - held
    if lines > used:
        pieces.append(jnp.zeros((lines - used, width), F32))
    out[held:, :] = jnp.concatenate(pieces, axis=0).astype(BF16)
    first.wait()


def gate_kernel(*refs):
    del refs


def filter_kernel(
    nranks, own, nzb, low, high, k0, k1, k2, *refs,
):
    k3, refs = refs[:SPLIT], refs[SPLIT:]
    (
        a0, a1, a2, a3, phi_out, theta_out, rs_out,
        yb, zs, scale, heavy, codes, pat, mine, psem, ksem,
    ) = refs
    fetch = pltpu.make_async_copy(k0, mine, ksem.at[0])
    fetch.start()
    ya = phi_out
    bs = k0.shape[1]
    nb = own * nranks
    held = own * bs
    me = lax.axis_index("split")
    kept = (mine, k1, k2)

    def rows_of(i):
        return pl.ds(i * bs if isinstance(i, int) else pl.multiple_of(i * bs, bs), bs)

    mass = []
    for t, ref in enumerate((a0, a1, a2, a3)):
        rows = ref[held:, :].astype(F32)
        codes[t * own : (t + 1) * own, :] = rows[3 * own : 4 * own, :].astype(jnp.int32)
        mass.append(rows[:own] + rows[own : 2 * own] + rows[2 * own : 3 * own])
    down = pltpu.make_async_copy(codes, pat, psem.at[0])
    down.start()
    for t, ref in enumerate((a0, a1, a2, a3)):
        ya[pl.ds(pl.multiple_of((me ^ t) * held, held), held), :] = ref[:held, :]
    centre = (high[0] + low[0]) / 2.0
    half = (high[0] - low[0]) / 2.0
    shift = jnp.full((1, 1), centre, F32) / half
    down.wait()

    def order():
        for t in range(nranks):
            for r in range(own):
                yield t, r, (me ^ t) * own + r

    def image(t, r, src):
        if t < 3:
            left = [kept[t][rows_of(r * nzb + k), :] for k in range(nzb)]
        else:
            per = own // SPLIT
            left = [k3[r // per][rows_of(r % per * nzb + k), :] for k in range(nzb)]
        left = jnp.concatenate(left, axis=1)
        right = jnp.concatenate([src[rows_of(pat[t * own + r, k]), :] for k in range(nzb)], axis=0)
        return jnp.dot(left, right, preferred_element_type=F32)

    for t, r, i in sorted(order(), key=lambda x: x[0] == 0):
        if (t, r) == (0, 0):
            fetch.wait()
        at = rows_of(i)
        row = jnp.broadcast_to(mass[t][r : r + 1, :], (bs, bs)).T
        heavy[at, :] = row
        scaled = 1.0 / (row * half)
        scale[at, :] = scaled
        yb[at, :] = (image(t, r, ya) * scaled - shift * ya[at, :].astype(F32)).astype(BF16)

    @pl.loop(0, ITERS)
    def _(it):
        src, dst = yb, ya
        for _ in range(DEG - 1):
            for t, r, i in order():
                at = rows_of(i)
                dst[at, :] = (
                    2.0 * (image(t, r, src) * scale[at, :] - shift * src[at, :].astype(F32))
                    - dst[at, :].astype(F32)
                ).astype(BF16)
            src, dst = dst, src
        cur = src
        gram = jnp.zeros((bs, bs), F32)
        for i in range(nb):
            blk = cur[rows_of(i), :]
            hi, lo = split2(blk.astype(F32) * heavy[rows_of(i), :])
            both = lax.dot_general(
                blk, jnp.concatenate([hi, lo], axis=1), (((0,), (0,)), ((), ())), preferred_element_type=F32
            )
            gram = gram + both[:, :bs] + both[:, bs:]
        todo = list(order())

        def between(b):
            for t, r, i in todo[nb * b // groups : nb * (b + 1) // groups]:
                zs[rows_of(i), :] = image(t, r, cur).astype(BF16)

        groups = bs // 8
        hi, lo = split2(inverse_factor(gram, between))
        twice = jnp.concatenate([hi, lo], axis=0)
        theta = jnp.zeros((8, bs), F32)
        for i in range(nb):
            at = rows_of(i)
            blk = cur[at, :]
            phi = jnp.dot(jnp.concatenate([blk, blk], axis=1), twice, preferred_element_type=F32).astype(BF16)
            blk = zs[at, :]
            img = jnp.dot(jnp.concatenate([blk, blk], axis=1), twice, preferred_element_type=F32)
            ya[at, :] = phi
            phi = phi.astype(F32)
            yb[at, :] = (img * scale[at, :] - shift * phi).astype(BF16)
            theta = theta + jnp.sum((phi * img).reshape(-1, 8, bs), axis=0)
        theta = jnp.sum(theta, axis=0, keepdims=True)
        theta_out[...] = theta
        rs_out[...] = jnp.broadcast_to(lax.rsqrt(theta), rs_out.shape)


def product_kernel(phi, rs, c0, c2, out):
    me = lax.axis_index("split")
    njs, bs, cols = c0.shape
    mine = phi[pl.ds(pl.multiple_of(me * cols, cols), cols), :]
    other = phi[pl.ds(pl.multiple_of((me ^ 2) * cols, cols), cols), :]
    right = jnp.concatenate([mine, other], axis=0)
    scale = rs[0:1, :]
    for j in range(njs):
        left = jnp.concatenate([c0[j], c2[j]], axis=1)
        out[j] = (jnp.dot(left, right, preferred_element_type=F32) * scale).astype(BF16)


def face_kernel(nranks, nsub, links, slots, mine, other, keep, send, dense):
    me = lax.axis_index("split")
    faces, share, _ = dense.shape
    first = lax.axis_index("sub") * (faces // nsub)
    dense[...] = jnp.zeros_like(dense)
    for j in range(mine.shape[0]):
        hi, lo = split2(mine[j].astype(F32) + other[j].astype(F32))
        left = jnp.concatenate([hi, lo, hi], axis=1)
        right = jnp.concatenate([hi, hi, lo], axis=1)
        rows = left[:share]
        for r in range(1, nranks):
            rows = jnp.where(me == r, left[share * r : share * (r + 1)], rows)
        dense[slots[links[0, j]] ^ first] = lax.dot_general(
            rows, right, (((1,), (1,)), ((), ())), preferred_element_type=F32
        )
    half = faces // 2
    keep[...] = dense[:half]
    send[...] = dense[half:].astype(BF16)


def shards(stiffness, pattern, mass, start_modes, cut_low, cut_high, coupling, incidence, slot_of):
    stiff = stiffness[0]
    own, nzb, bs, _ = stiff.shape
    modes = start_modes.shape[-1]
    nranks = lax.axis_size("split")
    nsub = lax.axis_size("sub")
    nb = own * nranks
    faces = slot_of.shape[0]
    assert nranks == 4 and nsub & (nsub - 1) == 0

    def swap(x, bits, axis="split", n=nranks):
        return lax.ppermute(x, axis, [(i, i ^ bits) for i in range(n)])

    smem = pl.BlockSpec(memory_space=pltpu.SMEM)
    vmem = pl.BlockSpec(memory_space=pltpu.VMEM)
    hbm = pl.BlockSpec(memory_space=pltpu.HBM)
    blocks = stiff.reshape(-1, bs)
    lines = -(-4 * own // 16) * 16
    a_0 = pl.pallas_call(
        pack_kernel,
        out_shape=jax.ShapeDtypeStruct((own * bs + lines, modes), BF16),
        in_specs=[hbm, vmem, vmem, hbm],
        out_specs=vmem,
        scratch_shapes=[pltpu.SemaphoreType.DMA((1,))],
        compiler_params=pltpu.CompilerParams(vmem_limit_bytes=GATE_VMEM),
        name="pack",
    )(start_modes[0], mass, pattern[0], blocks)
    k_2 = swap(blocks, 2)
    k_1 = swap(blocks, 1)
    a_2 = swap(a_0, 2)
    a_1 = swap(a_0, 1)
    a_2 = pl.pallas_call(
        gate_kernel,
        out_shape=jax.ShapeDtypeStruct(a_2.shape, a_2.dtype),
        in_specs=[hbm] * 2,
        out_specs=hbm,
        input_output_aliases={0: 0},
        compiler_params=pltpu.CompilerParams(vmem_limit_bytes=GATE_VMEM),
        name="gate",
    )(a_2, a_1)
    a_3 = swap(a_2, 1)
    a_3 = pl.pallas_call(
        gate_kernel,
        out_shape=jax.ShapeDtypeStruct(a_3.shape, a_3.dtype),
        in_specs=[hbm],
        out_specs=hbm,
        input_output_aliases={0: 0},
        compiler_params=pltpu.CompilerParams(vmem_limit_bytes=GATE_VMEM),
        cost_estimate=pl.CostEstimate(flops=XFLOPS, bytes_accessed=0, transcendentals=0),
        name="gate",
    )(a_3)
    part = k_2.shape[0] // SPLIT
    k_3 = [swap(k_2[i * part : (i + 1) * part], 1) for i in range(SPLIT)]
    c_2 = swap(coupling[0], 2)

    phi, theta, rs = pl.pallas_call(
        functools.partial(filter_kernel, nranks, own, nzb),
        out_shape=(
            jax.ShapeDtypeStruct((nb * bs, modes), BF16),
            jax.ShapeDtypeStruct((1, modes), F32),
            jax.ShapeDtypeStruct((8, modes), F32),
        ),
        in_specs=[smem, smem, hbm] + [vmem] * (6 + SPLIT),
        out_specs=(vmem, vmem, vmem),
        scratch_shapes=[
            pltpu.VMEM((nb * bs, modes), BF16),
            pltpu.VMEM((nb * bs, modes), BF16),
            pltpu.VMEM((nb * bs, modes), F32),
            pltpu.VMEM((nb * bs, modes), F32),
            pltpu.VMEM((nb, modes), jnp.int32),
            pltpu.SMEM((nb, modes), jnp.int32),
            pltpu.VMEM(blocks.shape, BF16),
            pltpu.SemaphoreType.DMA((1,)),
            pltpu.SemaphoreType.DMA((1,)),
        ],
        compiler_params=pltpu.CompilerParams(vmem_limit_bytes=FILTER_VMEM),
        cost_estimate=pl.CostEstimate(flops=FFLOPS, bytes_accessed=8 << 20, transcendentals=0),
        name="filter",
    )(cut_low, cut_high, blocks, k_1, k_2, *k_3, a_0, a_1, a_2, a_3)

    share = bs // nranks
    nif = coupling.shape[1]
    prods = pl.pallas_call(
        product_kernel,
        out_shape=jax.ShapeDtypeStruct((nif, bs, modes), BF16),
        in_specs=[vmem] * 4,
        out_specs=vmem,
        compiler_params=pltpu.CompilerParams(vmem_limit_bytes=16 << 20),
        name="products",
    )(phi, rs, coupling[0], c_2)
    total, send = pl.pallas_call(
        functools.partial(face_kernel, nranks, nsub),
        out_shape=(
            jax.ShapeDtypeStruct((faces // 2, share, bs), F32),
            jax.ShapeDtypeStruct((faces // 2, share, bs), BF16),
        ),
        in_specs=[smem, smem, vmem, vmem],
        out_specs=(vmem, vmem),
        scratch_shapes=[pltpu.VMEM((faces, share, bs), F32)],
        compiler_params=pltpu.CompilerParams(vmem_limit_bytes=16 << 20),
        name="faces",
    )(incidence, slot_of, prods, swap(prods, 1))
    width = nsub // 2
    while True:
        total = total + swap(send, width, "sub", nsub).astype(F32)
        width //= 2
        if not width:
            break
        at = total.shape[0] // 2
        total, send = total[:at], total[at:].astype(BF16)
    return (total, theta)


def solution(mesh):
    placed = (
        P("sub", "split", None, None, None),
        P("sub", "split", None),
        P("sub", "split"),
        P("sub", "split", None),
        P("sub"),
        P("sub"),
        P("sub", None, None, "split"),
        P("sub", None),
        P(),
    )
    return jax.shard_map(
        shards,
        mesh=mesh,
        in_specs=placed,
        out_specs=(P("sub", "split", None), P("sub", None)),
        check_vma=False,
    )
```
